512 devices in a mesh: dp: 2 (over y_hi), ctx: 32 (over z, y_lo), tp: 8 (over x, core).
Axes of the slice: x: 4, y: 4 (y_hi: 2, y_lo: 2; y = y_hi * 2 + y_lo), z: 16, core: 2. Of those that a mesh axis runs over, the one named last changes fastest.
Arguments:
- queries: bfloat16 [16384, 8192], P(('dp', 'ctx'), 'tp'), parts along dimension 0
- keys: bfloat16 [16384, 1024], P(('dp', 'ctx'), 'tp'), parts along dimension 0
- values: bfloat16 [16384, 1024], P(('dp', 'ctx'), 'tp'), parts along dimension 0, may hold values from -6 to 6
- query_norm_gain: float32 [128], replicated, may hold values from 0.1 to 1.9
- key_norm_gain: float32 [128], replicated, may hold values from 0.1 to 1.9
- positions: int32 [16384], P(('dp', 'ctx')), parts along dimension 0, may hold values from 0 to 4607, as said below
- segment_ids: int32 [16384], P(('dp', 'ctx')), parts along dimension 0, may hold values from 0 to 16, as said below
- block_mask: int32 [128, 64], P(('dp', 'ctx')), parts along dimension 0, may hold values from 0 to 1, as said below
Outputs:
- attended: bfloat16 [16384, 8192], P(('dp', 'ctx'), 'tp'), parts along dimension 0
The draws below stay inside these ranges and needn't reach their ends.
There are 2 independent parts, one for each index of `dp`. The reference program is written for one: setup_inputs(seed, part) draws one part's arguments, and reference() takes and returns one part's arrays. A program takes and returns all parts, laid end to end along the dimension named above; an argument that names none is the same for every part. Nothing has to cross between parts.
Inputs may be any that keep to these rules, and one draw needn't show every extreme that they name: segment_ids is 0 on the first 4096 tokens; then the responses 1 to 16 follow in order, each one contiguous run of 1 to 512 tokens, one of exactly 512, the last ending at the pack's end. `positions`: a prompt token's position is its index; a response token's is 4096 plus its offset in its response. block_mask[a, b] is 1 exactly when some token of block a may see some token of block b under the token rule, else 0.
All inputs are finite; a program needn't handle non-finite values.
Results may differ from the reference program's by a relative error of at most 0.0073.
Values may be sent and summed in bfloat16 or wider, within the bound.
No kernel may reach another device: no remote copies, remote signals or barrier semaphores. Data moves between devices by JAX's collectives and lax.ppermute only.
A program may use at most 64 MiB of HBM per device.

```python
import math
import jax
import jax.numpy as jnp
from jax import lax

HEAD_DIMENSION = 128
QUERY_PER_KEY = 8
KEY_VALUE_HEADS = 8
QUERY_HEADS = 64
BLOCK = 128
RESPONSES = 16
PACK_TOKENS = 8192
PROMPT = 4096
MOST = 512
NB = 64


def response_lengths(key):
    key = jax.random.fold_in(key, 11)
    first_key, second_key = jax.random.split(key)
    rest = PACK_TOKENS // 2 - MOST
    base_frequency = rest // 15
    extra = rest % 15
    spread = max(0, min(base_frequency - 1, MOST - base_frequency - 2))
    others = base_frequency + (jnp.arange(15) < extra).astype(jnp.int32)
    shifts = jax.random.randint(first_key, (7,), -spread, spread + 1).astype(jnp.int32)
    delta = jnp.zeros((15,), jnp.int32).at[0:14:2].add(shifts).at[1:14:2].add(-shifts)
    others = others + delta
    lengths = jnp.concatenate([jnp.full((1,), MOST, jnp.int32), others])
    order = jax.random.permutation(second_key, RESPONSES)
    return lengths[order]


def token_layout(key):
    lengths = response_lengths(key)
    starts = PROMPT + jnp.cumsum(lengths) - lengths
    token = jnp.arange(PACK_TOKENS, dtype=jnp.int32)
    segment = jnp.sum((token[:, None] >= starts[None, :]).astype(jnp.int32), axis=1).astype(jnp.int32)
    begin = starts[jnp.maximum(segment - 1, 0)]
    place = jnp.where(segment == 0, token, PROMPT + token - begin).astype(jnp.int32)
    return (segment, place)


def draw_segment_ids(key, part):
    segment, place = token_layout(key)
    return segment


def draw_positions(key, part):
    segment, place = token_layout(key)
    return place


def draw_block_mask(key, part):
    segment, place = token_layout(key)
    grid = segment.reshape(NB, BLOCK)
    first = grid[:, 0]
    last = grid[:, BLOCK - 1]
    row = jnp.arange(NB, dtype=jnp.int32)[:, None]
    col = jnp.arange(NB, dtype=jnp.int32)[None, :]
    intersection = (first[None, :] <= last[:, None]) & (first[:, None] <= last[None, :])
    seen = (col <= row) & ((col * BLOCK < PROMPT) | intersection)
    return seen.astype(jnp.int32)


def draw_queries(key, part):
    key = jax.random.fold_in(key, 5)
    base_key, row_key, column_key_seed = jax.random.split(key, 3)
    array_shape = (PACK_TOKENS, QUERY_HEADS * HEAD_DIMENSION)
    base_frequency = jax.random.normal(base_key, array_shape, jnp.float32)
    upper_bound = math.log(10.0)
    row_scale = jnp.exp(jax.random.uniform(row_key, (PACK_TOKENS, 1), jnp.float32, 0.0, upper_bound))
    column_weight_scale = jnp.exp(jax.random.uniform(column_key_seed, (1, QUERY_HEADS * HEAD_DIMENSION), jnp.float32, 0.0, upper_bound))
    return (base_frequency * row_scale * column_weight_scale * 0.3).astype(jnp.bfloat16)


def draw_keys(key, part):
    key = jax.random.fold_in(key, 7)
    base_key, row_key, column_key_seed = jax.random.split(key, 3)
    array_shape = (PACK_TOKENS, KEY_VALUE_HEADS * HEAD_DIMENSION)
    base_frequency = jax.random.normal(base_key, array_shape, jnp.float32)
    upper_bound = math.log(10.0)
    row_scale = jnp.exp(jax.random.uniform(row_key, (PACK_TOKENS, 1), jnp.float32, 0.0, upper_bound))
    column_weight_scale = jnp.exp(jax.random.uniform(column_key_seed, (1, KEY_VALUE_HEADS * HEAD_DIMENSION), jnp.float32, 0.0, upper_bound))
    return (base_frequency * row_scale * column_weight_scale * 0.3).astype(jnp.bfloat16)


def block_levels(key, extent, cuts, least, largest):
    def one(axis_at, shards_of):
        steps = jax.random.uniform(jax.random.fold_in(jax.random.fold_in(key, 6), axis_at), (shards_of,), jnp.float32, least / len(cuts), largest / len(cuts))
        return jnp.repeat(jnp.exp(steps), extent[axis_at] // shards_of).reshape((-1,) + (1,) * (len(extent) - axis_at - 1))

    level = one(*cuts[0])
    for cut in cuts[1:]:
        level = level * one(*cut)
    return level


def bell_draw(rng, dims, width, reach, cuts=(), kind=jnp.bfloat16):
    result = jax.random.normal(rng, dims, jnp.float32) * width
    if len(cuts) > 0:
        result = block_levels(rng, dims, cuts, -0.22, 0.18) * result
    return jnp.clip(result, min=-reach, max=reach).astype(kind)


def setup_inputs(seed: int = 0, part: int = 0) -> dict:
    key_list = jax.random.split(jax.random.key(seed), 9)
    part_splits = jax.random.split(jax.random.fold_in(key_list[8], part), 9)
    return {
        "queries": draw_queries(jax.random.fold_in(jax.random.fold_in(key_list[8], part), 71), part),
        "keys": draw_keys(jax.random.fold_in(jax.random.fold_in(key_list[8], part), 71), part),
        "values": bell_draw(part_splits[2], (PACK_TOKENS, KEY_VALUE_HEADS * HEAD_DIMENSION), 1.0, 6.0, ((0, 32), (1, 8))),
        "query_norm_gain": jnp.clip(1.0 + 0.18 * jax.random.normal(key_list[3], (HEAD_DIMENSION,), jnp.float32), 0.1, 1.9),
        "key_norm_gain": jnp.clip(1.0 + 0.18 * jax.random.normal(key_list[4], (HEAD_DIMENSION,), jnp.float32), 0.1, 1.9),
        "positions": draw_positions(jax.random.fold_in(jax.random.fold_in(key_list[8], part), 71), part),
        "segment_ids": draw_segment_ids(jax.random.fold_in(jax.random.fold_in(key_list[8], part), 71), part),
        "block_mask": draw_block_mask(jax.random.fold_in(jax.random.fold_in(key_list[8], part), 71), part),
    }


def apply_rotary_embedding(source, gain, positions, heads):
    count = source.shape[0]
    size = gain.shape[0]
    vec = source.astype(jnp.float32).reshape(count, heads, size)
    vec = vec * lax.rsqrt(lax.optimization_barrier(jnp.mean(vec * vec, axis=-1, keepdims=True)) + 1e-06) * gain
    half = size // 2
    freq = jnp.exp(-math.log(1000000.0) * jnp.arange(half, dtype=jnp.float32) * (2.0 / size))
    angle = positions.astype(jnp.float32)[:, None] * freq[None, :]
    cosine = jnp.cos(angle)[:, None, :]
    sine = jnp.sin(angle)[:, None, :]
    first = vec[..., :half]
    second = vec[..., half:]
    out = jnp.concatenate([first * cosine - second * sine, second * cosine + first * sine], axis=-1)
    return out.astype(jnp.bfloat16)

def reference(queries, keys, values, query_norm_gain, key_norm_gain, positions, segment_ids, block_mask):
    query_rotated_rows = apply_rotary_embedding(queries, query_norm_gain, positions, QUERY_HEADS).reshape(PACK_TOKENS, KEY_VALUE_HEADS, QUERY_PER_KEY, HEAD_DIMENSION)
    key_rotated_rows = apply_rotary_embedding(keys, key_norm_gain, positions, KEY_VALUE_HEADS)
    value_entries = values.reshape(PACK_TOKENS, KEY_VALUE_HEADS, HEAD_DIMENSION)
    key_index = jnp.arange(PACK_TOKENS, dtype=jnp.int32)
    qblk = math.gcd(PACK_TOKENS, 1024)
    scale = HEAD_DIMENSION ** (-0.5)

    def one_block(index):
        start = (index * qblk).astype(jnp.int32)
        query_index = start + jnp.arange(qblk, dtype=jnp.int32)
        qpart = lax.dynamic_slice_in_dim(query_rotated_rows, start, qblk, 0)
        qseg = lax.dynamic_slice_in_dim(segment_ids, start, qblk, 0)
        rows_tab = lax.dynamic_slice_in_dim(block_mask, (start // BLOCK).astype(jnp.int32), qblk // BLOCK, 0)
        live = jnp.repeat(jnp.repeat(rows_tab, BLOCK, axis=0), BLOCK, axis=1)
        mask = (live > 0) & (key_index[None, :] <= query_index[:, None])
        mask = mask & ((key_index < PROMPT)[None, :] | (segment_ids[None, :] == qseg[:, None]))

        def head_split_rows(head):
            qhead = qpart[:, head].astype(jnp.float32)
            khead = key_rotated_rows[:, head].astype(jnp.float32)
            vhead = value_entries[:, head].astype(jnp.float32)
            score = jnp.einsum('qgd,jd->gqj', qhead, khead) * scale
            weight = jnp.where(mask[None], jnp.exp(score), jnp.float32(0.0))
            total = lax.optimization_barrier(jnp.sum(weight, axis=-1))
            rounded = lax.optimization_barrier(weight.astype(jnp.bfloat16)).astype(jnp.float32)
            acc = jnp.einsum('gqj,jd->gqd', rounded, vhead)
            return (acc / total[..., None]).astype(jnp.bfloat16)
        head_outputs = lax.map(head_split_rows, jnp.arange(KEY_VALUE_HEADS, dtype=jnp.int32))
        return jnp.transpose(head_outputs, (2, 0, 1, 3)).reshape(qblk, QUERY_HEADS * HEAD_DIMENSION)
    blocks = lax.map(one_block, jnp.arange(PACK_TOKENS // qblk, dtype=jnp.int32))
    return blocks.reshape(PACK_TOKENS, QUERY_HEADS * HEAD_DIMENSION)
```

```python
import functools
import math

import jax
import jax.numpy as jnp
from jax import lax
from jax.experimental import pallas as pl
from jax.experimental.pallas import tpu as pltpu
from jax.sharding import PartitionSpec as P

HEAD = 128
NT = (((1,), (1,)), ((), ()))
VMEM = pl.BlockSpec(memory_space=pltpu.VMEM)
SMEM = pl.BlockSpec(memory_space=pltpu.SMEM)
PARAMS = pltpu.CompilerParams(vmem_limit_bytes=40 * 2**20)
PAD = 16

NEAR, HELD, LOW, HIGH, SKIP, MASKS = 2, 5, 7, 9, 11, 13


def rotate(vec, gain, cosine, sine):
    vec = vec.astype(jnp.float32)
    vec = vec * lax.rsqrt(jnp.mean(vec * vec, axis=-1, keepdims=True) + 1e-06) * gain
    turned = jnp.concatenate([vec[:, HEAD // 2 :], vec[:, : HEAD // 2]], axis=1)
    return vec * cosine + turned * sine


def key_kernel(keys, values, gain, cosine, sine, out):
    rows = keys.shape[0]
    out[:rows, :] = rotate(keys[...], gain[...], cosine[...], sine[...]).astype(out.dtype)
    out[rows:, :] = values[...]


def query_kernel(queries, gain, cosine, sine, mask, out):
    rows = queries.shape[0]
    heads = queries.shape[1] // HEAD
    for head in range(heads):
        part = queries[:, head * HEAD : (head + 1) * HEAD]
        out[head * rows : (head + 1) * rows, :] = rotate(
            part, gain[...], cosine[...], sine[...]
        ).astype(out.dtype)
    out[heads * rows :, :] = jnp.broadcast_to(
        mask[...].astype(jnp.float32), (PAD, HEAD)
    ).astype(out.dtype)


def hold_kernel(info, own, far, below, above, held, *, period):
    plane = info[0] // 2
    size = own.shape[0]

    @pl.when(plane < period)
    def _():
        held[:size, :] = own[...]

    @pl.when(plane >= period)
    def _():
        held[:size, :] = far[...]

    middle = (plane >= period // 2) & (plane < period + period // 2)

    @pl.when(middle)
    def _():
        held[size:, :] = below[...]

    @pl.when(jnp.logical_not(middle))
    def _():
        held[size:, :] = above[...]


def attend_kernel(info, *refs, jobs, near, counts, rows, heads, prompt):
    refs = list(refs)
    starts = refs.pop(0) if near else None
    queries = [refs.pop(0) for _ in jobs]
    states = [refs.pop(0) if job["state"] else None for job in jobs]
    shards = []
    for count in counts:
        ref = refs.pop(0)
        shards += [(ref, part * 2 * rows) for part in range(count)]
    half = rows // 2
    scale = HEAD**-0.5 * math.log2(math.e)
    ones = jnp.ones((rows, HEAD), jnp.bfloat16)

    def partial(query, head, shard, mask):
        ref, at = shard
        score = lax.dot_general(
            query[pl.ds(head * rows, rows), :],
            ref[at : at + rows, :],
            NT,
            preferred_element_type=jnp.float32,
        )
        weight = jnp.exp2(score * scale)
        if mask is not None:
            weight = jnp.where(mask, weight, 0.0)
        extended = jnp.concatenate([ref[at + rows : at + 2 * rows, :], ones], axis=1)
        return jnp.dot(weight.astype(jnp.bfloat16), extended, preferred_element_type=jnp.float32)

    for job, query, state in zip(jobs, queries, states):
        out = refs.pop(0)
        total = refs.pop() if job["pack"] else out
        lane = job["lane"]
        mine = info[lane]

        def block(shard, a, b, lane=lane):
            width = 4 * prompt // rows
            return info[MASKS + lane * 2 * width + a * width + 2 * shard + b]

        some, full = [], []
        for slot in job["slots"]:
            shard = info[slot]
            seen = [block(shard, a, b) > 0 for a in range(2) for b in range(2)]
            any_seen = seen[0] | seen[1] | seen[2] | seen[3]
            if near:
                any_seen = any_seen & (shard * rows >= prompt)
            some.append(any_seen)
            full.append(
                seen[0]
                & seen[1]
                & seen[2]
                & seen[3]
                & (shard < mine)
                & (shard * rows < prompt)
            )
        all_full = functools.reduce(jnp.logical_and, full)

        def together(query=query, state=state, total=total):
            for head in range(heads):
                at = pl.ds(head * rows, rows)
                add = None if state is None else state[at, :]
                for shard in shards:
                    new = partial(query, head, shard, None)
                    add = new if add is None else add + new
                total[at, :] = add

        def one_by_one(
            job=job, query=query, state=state, total=total, mine=mine, some=some, full=full, block=block
        ):
            total[...] = jnp.zeros_like(total) if state is None else state[...]
            for slot, shard, any_seen, all_seen in zip(job["slots"], shards, some, full):

                def add(mask, query=query, shard=shard, total=total):
                    @pl.loop(0, heads // 4)
                    def _(group):
                        for inner in range(4):
                            head = group * 4 + inner
                            at = pl.ds(pl.multiple_of(head * rows, rows), rows)
                            total[at, :] += partial(query, head, shard, mask)

                if not near:

                    @pl.when(all_seen)
                    def _(add=add):
                        add(None)

                @pl.when(any_seen & jnp.logical_not(all_seen))
                def _(slot=slot, add=add):
                    number = info[slot]
                    row = lax.broadcasted_iota(jnp.int32, (rows, rows), 0)
                    column = lax.broadcasted_iota(jnp.int32, (rows, rows), 1)
                    upper = jnp.where(column < half, block(number, 0, 0), block(number, 0, 1))
                    lower = jnp.where(column < half, block(number, 1, 0), block(number, 1, 1))
                    key = number * rows + column
                    mask = (jnp.where(row < half, upper, lower) > 0) & (key <= mine * rows + row)
                    if near:
                        begun = jnp.concatenate([starts[...]] * (rows // HEAD), axis=1)
                        mask = mask & ((key < prompt) | (key >= begun))
                    add(mask)

        if near:
            one_by_one()
        else:
            pl.when(all_full)(together)
            pl.when(jnp.logical_not(all_full))(one_by_one)

        if job["pack"]:
            at_lane = lax.broadcasted_iota(jnp.int32, (rows, HEAD), 1)
            packed = jnp.zeros((rows, HEAD), jnp.float32)
            for head in range(heads):
                at = pl.ds(head * rows, rows)
                out[at, :] = total[at, :HEAD].astype(out.dtype)
                whole = total[at, HEAD:]
                high = whole.astype(jnp.bfloat16).astype(jnp.float32)
                packed = jnp.where(at_lane == head, high, packed)
                packed = jnp.where(at_lane == heads + head, whole - high, packed)
            out[heads * rows :, :] = packed.astype(out.dtype)


def finish_kernel(own, other, out):
    rows = out.shape[0]
    heads = out.shape[1] // HEAD
    packed = other[heads * rows :, :]
    source = lax.broadcasted_iota(jnp.int32, (HEAD, HEAD), 0)
    for head in range(heads):
        at = slice(head * rows, (head + 1) * rows)
        pick = jnp.where((source == head) | (source == heads + head), 1.0, 0.0)
        total = jnp.dot(packed, pick.astype(jnp.bfloat16), preferred_element_type=jnp.float32)
        total = total + own[at, HEAD:]
        value = own[at, :HEAD] + other[at, :].astype(jnp.float32)
        out[:, head * HEAD : (head + 1) * HEAD] = (value / total).astype(out.dtype)


def local(
    queries, keys, values, query_norm_gain, key_norm_gain, positions, segment_ids, block_mask
):
    rows = queries.shape[0]
    heads = queries.shape[1] // HEAD
    ring = lax.axis_size("ctx")
    mine = lax.axis_index("ctx")
    prompt = ring * rows // 2
    depth = ring // 2
    period = depth // 2
    plane, lane = mine // 2, mine % 2
    shape = jax.ShapeDtypeStruct

    def move(array, target):
        pairs = [(z * 2 + y, target(z) % depth * 2 + y) for z in range(depth) for y in range(2) if target(z) is not None]
        return lax.ppermute(array, "ctx", pairs)

    def swap(array):
        return lax.ppermute(array, "ctx", [(c, c ^ 1) for c in range(ring)])

    with jax.named_scope("angles"):
        freq = jnp.exp(
            -math.log(1000000.0) * jnp.arange(HEAD // 2, dtype=jnp.float32) * (2.0 / HEAD)
        )
        freq = jnp.concatenate([freq, freq])
        angle = positions.astype(jnp.float32)[:, None] * freq[None, :]
        sign = jnp.where(jnp.arange(HEAD) < HEAD // 2, -1.0, 1.0).astype(jnp.float32)
        cosine = jnp.cos(angle)
        sine = jnp.sin(angle) * sign[None, :]

    def whole(array_shape):
        return pl.BlockSpec(array_shape, lambda i: (0,) * len(array_shape))

    kv = pl.pallas_call(
        key_kernel,
        grid=(1,),
        out_shape=shape((2 * rows, HEAD), jnp.bfloat16),
        in_specs=[whole((rows, HEAD))] * 2 + [whole((1, HEAD))] + [whole((rows, HEAD))] * 2,
        out_specs=whole((2 * rows, HEAD)),
        compiler_params=PARAMS,
        name="rotate_keys",
    )(keys, values, key_norm_gain[None, :], cosine, sine)

    far = move(kv, lambda z: z + period if z < period else None)
    below = move(kv, lambda z: z + period // 2 if z < period else None)
    above = move(kv, lambda z: z - period // 2 if z < period else None)

    query = pl.pallas_call(
        query_kernel,
        grid=(1,),
        out_shape=shape((heads * rows + PAD, HEAD), jnp.bfloat16),
        in_specs=[whole((rows, heads * HEAD)), whole((1, HEAD))]
        + [whole((rows, HEAD))] * 2
        + [whole((1, HEAD))],
        out_specs=whole((heads * rows + PAD, HEAD)),
        compiler_params=PARAMS,
        name="rotate_queries",
    )(queries, query_norm_gain[None, :], cosine, sine, block_mask.reshape(1, HEAD))
    query_cross = swap(query)

    near1 = lax.ppermute(kv, "ctx", [(c, c + 1) for c in range(ring // 2, ring - 1)])
    near2 = lax.ppermute(kv, "ctx", [(c, c + 2) for c in range(ring // 2, ring - 2)])

    def number(offset):
        return (plane + offset) % period * 2 + lane

    odd = plane % 2
    numbers = [mine, mine + 1 - 2 * lane, mine, mine - 1, mine - 2]
    numbers += [number(o) for o in (0, 4, -1, 3, 1, 5)]
    numbers += [number(2 + 4 * odd), number(6 - 4 * odd)]
    numbers = jnp.stack(numbers).astype(jnp.int32)
    info_own = jnp.concatenate([numbers, block_mask.reshape(-1)])
    index = mine * rows + jnp.arange(rows, dtype=jnp.int32)
    starts = jnp.broadcast_to((index - (positions - prompt))[:, None], (rows, HEAD))

    def attend(info, jobs, queries_in, states, shards, counts, name, near=False):
        out_shape, scratch = [], []
        for job in jobs:
            sums = shape((heads * rows, 2 * HEAD), jnp.float32)
            if job["pack"]:
                scratch.append(pltpu.VMEM(sums.shape, sums.dtype))
                sums = shape((heads * rows + rows, HEAD), jnp.bfloat16)
            out_shape.append(sums)
        inputs = [info] + ([starts] if near else []) + queries_in + states + shards
        work = heads * rows * rows * sum(len(job["slots"]) for job in jobs)
        return pl.pallas_call(
            functools.partial(
                attend_kernel,
                jobs=jobs,
                near=near,
                counts=counts,
                rows=rows,
                heads=heads,
                prompt=prompt,
            ),
            out_shape=out_shape,
            in_specs=[SMEM] + [VMEM] * (len(inputs) - 1),
            out_specs=[VMEM] * len(out_shape),
            scratch_shapes=scratch,
            cost_estimate=pl.CostEstimate(
                flops=8 * HEAD * work, bytes_accessed=4 * heads * rows * HEAD, transcendentals=work
            ),
            compiler_params=PARAMS,
            name=name,
        )(*inputs)

    def job(lane, slots, state, pack=False):
        return dict(lane=lane, slots=slots, state=state, pack=pack)

    (own,) = attend(
        info_own,
        [job(0, [NEAR, NEAR + 1, NEAR + 2], False)],
        [query],
        [],
        [kv, near1, near2],
        [1, 1, 1],
        "attend_near",
        near=True,
    )
    mask_cross = query_cross[heads * rows, :].astype(jnp.int32)
    info = jnp.concatenate([info_own, mask_cross])
    far, below, above, own, query_cross, info = lax.optimization_barrier(
        (far, below, above, own, query_cross, info)
    )

    held = pl.pallas_call(
        functools.partial(hold_kernel, period=period),
        out_shape=shape((4 * rows, HEAD), jnp.bfloat16),
        in_specs=[SMEM] + [VMEM] * 4,
        out_specs=VMEM,
        compiler_params=PARAMS,
        name="hold_shards",
    )(info_own, kv, far, below, above)
    low = move(held, lambda z: z + 1)
    high = move(held, lambda z: z - 1)
    skip = move(held, lambda z: z + 2 if z % 2 else z - 2)

    slots = [HELD, HELD + 1]
    own, cross = attend(
        info,
        [job(0, slots, True), job(1, slots, False)],
        [query, query_cross],
        [own],
        [held],
        [2],
        "attend_held",
    )
    slots = [LOW, LOW + 1, HIGH, HIGH + 1]
    (cross,) = attend(
        info, [job(1, slots, True)], [query_cross], [cross], [low, high], [2, 2], "attend_next_cross"
    )
    last = [SKIP, SKIP + 1]
    (cross,) = attend(
        info, [job(1, last, True, True)], [query_cross], [cross], [skip], [2], "attend_last_cross"
    )
    other = swap(cross)
    (own,) = attend(
        info,
        [job(0, slots + last, True)],
        [query],
        [own],
        [low, high, skip],
        [2, 2, 2],
        "attend_last",
    )
    return pl.pallas_call(
        finish_kernel,
        out_shape=shape((rows, heads * HEAD), jnp.bfloat16),
        in_specs=[VMEM] * 2,
        out_specs=VMEM,
        compiler_params=PARAMS,
        name="finish",
    )(own, other)


def solution(mesh):
    return jax.shard_map(
        local,
        mesh=mesh,
        in_specs=(
            P(("dp", "ctx"), "tp"),
            P(("dp", "ctx"), "tp"),
            P(("dp", "ctx"), "tp"),
            P(),
            P(),
            P(("dp", "ctx")),
            P(("dp", "ctx")),
            P(("dp", "ctx"), None),
        ),
        out_specs=P(("dp", "ctx"), "tp"),
        check_vma=False,
    )
```

```python
import functools
import math

import jax
import jax.numpy as jnp
import numpy as np
from jax import lax
from jax.experimental import pallas as pl
from jax.experimental.pallas import tpu as pltpu
from jax.sharding import PartitionSpec as P

HEAD = 128
NT = (((1,), (1,)), ((), ()))
HBM = pl.BlockSpec(memory_space=pltpu.HBM)
VMEM = pl.BlockSpec(memory_space=pltpu.VMEM)
SMEM = pl.BlockSpec(memory_space=pltpu.SMEM)
PARAMS = pltpu.CompilerParams(vmem_limit_bytes=40 * 2**20)
COST = pl.CostEstimate(flops=1, bytes_accessed=1, transcendentals=0)
CHOOSE = 10**10
PAD = 16
PART = 128

NEAR, HELD, LOW, HIGH, SKIP, MASKS = 2, 4, 6, 8, 10, 12


def rotate(vec, gain, cosine, sine):
    vec = vec.astype(jnp.float32)
    vec = vec * lax.rsqrt(jnp.mean(vec * vec, axis=-1, keepdims=True) + 1e-06) * gain
    turned = jnp.concatenate([vec[:, HEAD // 2 :], vec[:, : HEAD // 2]], axis=1)
    return vec * cosine + turned * sine


def cos_sin(angle):
    turns = jnp.floor(angle * (2 / math.pi) + 0.5)
    rest = angle - turns * 1.5703125
    rest = rest - turns * 4.837512969970703e-4
    rest = rest - turns * 7.549789954891882e-8
    square = rest * rest
    sine = -1.9515295891e-4 * square + 8.3321608736e-3
    sine = (sine * square - 1.6666654611e-1) * square * rest + rest
    cosine = 2.443315711809948e-5 * square - 1.388731625493765e-3
    cosine = (cosine * square + 4.166664568298827e-2) * square * square - 0.5 * square + 1.0
    quarter = turns.astype(jnp.int32)
    odd = (quarter & 1) == 1
    swapped_sine = jnp.where(odd, cosine, sine)
    swapped_cosine = jnp.where(odd, sine, cosine)
    sine = jnp.where((quarter & 2) == 2, -swapped_sine, swapped_sine)
    cosine = jnp.where(((quarter + 1) & 2) == 2, -swapped_cosine, swapped_cosine)
    return cosine, sine


def key_kernel(keys, values, gain, positions, freq, out, cosine, sine, key_at, gain_at, pos_at, freq_at, sems):
    rows = keys.shape[0]
    copies = [
        pltpu.make_async_copy(source, target, sems.at[i])
        for i, (source, target) in enumerate(
            [
                (positions, pos_at),
                (freq, freq_at),
                (keys, key_at),
                (gain, gain_at),
                (values, out.at[pl.ds(rows, rows), :]),
            ]
        )
    ]
    for copy in copies:
        copy.start()
    copies[0].wait()
    copies[1].wait()
    place = jnp.broadcast_to(pos_at[...].astype(jnp.float32), (HEAD, rows)).T
    cos, sin = cos_sin(place * freq_at[...])
    lane = lax.broadcasted_iota(jnp.int32, (rows, HEAD), 1)
    sin = jnp.where(lane < HEAD // 2, -sin, sin)
    cosine[...] = cos
    sine[...] = sin
    copies[2].wait()
    copies[3].wait()
    out[:rows, :] = rotate(key_at[...], gain_at[...], cos, sin).astype(out.dtype)
    copies[4].wait()


def query_kernel(
    queries, gain, cosine, sine, mask, positions, out, query_at, gain_at, cos_at, sin_at, mask_at, pos_at, sems
):
    rows = queries.shape[0]
    heads = queries.shape[1] // HEAD
    sources = [mask, positions, gain, cosine, sine, queries]
    targets = [mask_at, pos_at, gain_at, cos_at, sin_at, query_at]
    copies = [
        pltpu.make_async_copy(source, target, sems.at[i])
        for i, (source, target) in enumerate(zip(sources, targets))
    ]
    for copy in copies:
        copy.start()
    copies[0].wait()
    copies[1].wait()
    line = mask_at[...].astype(jnp.float32)
    place = pos_at[...]
    high = (place >> 7).astype(jnp.float32)
    low = (place & (PART - 1)).astype(jnp.float32)
    lines = [jnp.concatenate([line[:1, :], line[1:, :]], axis=1)]
    lines += [part[:, at : at + HEAD] for part in (high, low) for at in range(0, rows, HEAD)]
    lines += [jnp.zeros((PAD - len(lines), HEAD), jnp.float32)]
    out[heads * rows :, :] = jnp.concatenate(lines, axis=0).astype(out.dtype)
    for copy in copies[2:]:
        copy.wait()
    for head in range(heads):
        part = query_at[:, head * HEAD : (head + 1) * HEAD]
        out[head * rows : (head + 1) * rows, :] = rotate(
            part, gain_at[...], cos_at[...], sin_at[...]
        ).astype(out.dtype)


def choose_kernel(info, inside, across, out, *, period):
    @pl.when(info[0] // 2 < period)
    def _():
        out[...] = inside[...]

    @pl.when(info[0] // 2 >= period)
    def _():
        out[...] = across[...]


def hold_kernel(info, own, opposite, second, held, *, period):
    size = own.shape[0]

    @pl.when(info[0] // 2 < period)
    def _():
        held[:size, :] = own[...]

    @pl.when(info[0] // 2 >= period)
    def _():
        held[:size, :] = second[...]

    held[size:, :] = opposite[...]


def attend_kernel(info, *refs, jobs, slots, counts, rows, heads, prompt):
    refs = list(refs)
    queries = [refs.pop(0) for _ in jobs]
    states = [refs.pop(0) if job["state"] else None for job in jobs]
    shards = []
    for count in counts:
        ref = refs.pop(0)
        shards += [(ref, part * 2 * rows) for part in range(count)]
    half = rows // 2
    scale = HEAD**-0.5 * math.log2(math.e)
    ones = jnp.ones((rows, HEAD), jnp.bfloat16)

    def partial(query, head, shard, mask):
        ref, at = shard
        score = lax.dot_general(
            query[pl.ds(head * rows, rows), :],
            ref[at : at + rows, :],
            NT,
            preferred_element_type=jnp.float32,
        )
        weight = jnp.exp2(score * scale)
        if mask is not None:
            weight = jnp.where(mask, weight, 0.0)
        extended = jnp.concatenate([ref[at + rows : at + 2 * rows, :], ones], axis=1)
        return jnp.dot(weight.astype(jnp.bfloat16), extended, preferred_element_type=jnp.float32)

    for job, query, state in zip(jobs, queries, states):
        out = refs.pop(0)
        total = refs.pop() if job["pack"] else out
        lane = job["lane"]
        mine = info[lane]

        def block(shard, a, b, lane=lane):
            width = 4 * prompt // rows
            return info[MASKS + lane * 2 * width + a * width + 2 * shard + b]

        early, late = [], []
        for (slot, near), shard in zip(slots, shards):
            number = info[slot]
            seen = [block(number, a, b) > 0 for a in range(2) for b in range(2)]
            any_seen = seen[0] | seen[1] | seen[2] | seen[3]
            if near:
                late.append((shard, number, any_seen & (number * rows >= prompt)))
            else:
                all_seen = seen[0] & seen[1] & seen[2] & seen[3]
                all_seen = all_seen & (number < mine) & (number * rows < prompt)
                early.append((shard, number, any_seen, all_seen))

        def add(shard, mask, query=query, total=total):
            @pl.loop(0, heads // 4)
            def _(group):
                for inner in range(4):
                    head = group * 4 + inner
                    at = pl.ds(pl.multiple_of(head * rows, rows), rows)
                    total[at, :] += partial(query, head, shard, mask)

        def add_masked(shard, number, near, add=add, block=block, query=query, mine=mine):
            row = lax.broadcasted_iota(jnp.int32, (rows, rows), 0)
            column = lax.broadcasted_iota(jnp.int32, (rows, rows), 1)
            upper = jnp.where(column < half, block(number, 0, 0), block(number, 0, 1))
            lower = jnp.where(column < half, block(number, 1, 0), block(number, 1, 1))
            key = number * rows + column
            mask = (jnp.where(row < half, upper, lower) > 0) & (key <= mine * rows + row)
            if near:
                lines = query[heads * rows :, :].astype(jnp.float32)
                count = rows // HEAD
                place = jnp.concatenate(
                    [lines[1 + i : 2 + i, :] * PART + lines[1 + count + i : 2 + count + i, :] for i in range(count)],
                    axis=1,
                )
                offset = jnp.broadcast_to(place - prompt, (rows, rows)).T.astype(jnp.int32)
                mask = mask & ((key < prompt) | (key >= mine * rows + row - offset))
            add(shard, mask)

        def together(query=query, state=state, total=total, early=early):
            for head in range(heads):
                at = pl.ds(head * rows, rows)
                sums = None if state is None else state[at, :]
                for shard, *_ in early:
                    new = partial(query, head, shard, None)
                    sums = new if sums is None else sums + new
                total[at, :] = sums

        def one_by_one(state=state, total=total, early=early, add=add, add_masked=add_masked):
            total[...] = jnp.zeros_like(total) if state is None else state[...]
            for shard, number, any_seen, all_seen in early:
                pl.when(all_seen)(functools.partial(add, shard, None))
                pl.when(any_seen & jnp.logical_not(all_seen))(
                    functools.partial(add_masked, shard, number, False)
                )

        if early:
            all_full = functools.reduce(jnp.logical_and, [entry[3] for entry in early])
            pl.when(all_full)(together)
            pl.when(jnp.logical_not(all_full))(one_by_one)
        else:
            one_by_one()
        for shard, number, any_seen in late:
            pl.when(any_seen)(functools.partial(add_masked, shard, number, True))

        if job["pack"]:
            at_lane = lax.broadcasted_iota(jnp.int32, (rows, HEAD), 1)
            packed = jnp.zeros((rows, HEAD), jnp.float32)
            for head in range(heads):
                at = pl.ds(head * rows, rows)
                out[at, :] = total[at, :HEAD].astype(out.dtype)
                whole = total[at, HEAD:]
                high = whole.astype(jnp.bfloat16).astype(jnp.float32)
                packed = jnp.where(at_lane == head, high, packed)
                packed = jnp.where(at_lane == heads + head, whole - high, packed)
            turned = packed.T[: 2 * heads, :].astype(out.dtype)
            for part in range(rows // HEAD):
                at = pl.ds(heads * rows + part * 2 * heads, 2 * heads)
                out[at, :] = turned[:, part * HEAD : (part + 1) * HEAD]


def finish_kernel(own, other, out):
    rows = out.shape[0]
    heads = out.shape[1] // HEAD
    base = heads * rows
    packed = jnp.concatenate(
        [other[base + p * 2 * heads : base + (p + 1) * 2 * heads, :] for p in range(rows // HEAD)],
        axis=1,
    )
    source = lax.broadcasted_iota(jnp.int32, (2 * heads, HEAD), 0)
    for head in range(heads):
        at = slice(head * rows, (head + 1) * rows)
        pick = jnp.where((source == head) | (source == heads + head), 1.0, 0.0)
        total = lax.dot_general(
            packed,
            pick.astype(jnp.bfloat16),
            (((0,), (0,)), ((), ())),
            preferred_element_type=jnp.float32,
        )
        total = total + own[at, HEAD:]
        value = own[at, :HEAD] + other[at, :].astype(jnp.float32)
        out[:, head * HEAD : (head + 1) * HEAD] = (value / total).astype(out.dtype)


def local(
    queries, keys, values, query_norm_gain, key_norm_gain, positions, segment_ids, block_mask
):
    rows = queries.shape[0]
    heads = queries.shape[1] // HEAD
    ring = lax.axis_size("ctx")
    mine = lax.axis_index("ctx")
    prompt = ring * rows // 2
    depth = ring // 2
    period = depth // 2
    plane, lane = mine // 2, mine % 2
    shape = jax.ShapeDtypeStruct

    def move(array, target):
        pairs = [(z * 2 + y, target(z) % depth * 2 + y) for z in range(depth) for y in range(2) if target(z) is not None]
        return lax.ppermute(array, "ctx", pairs)

    def swap(array):
        return lax.ppermute(array, "ctx", [(c, c ^ 1) for c in range(ring)])

    freq = 1000000.0 ** (-2.0 * (np.arange(HEAD) % (HEAD // 2)) / HEAD)
    freq = jnp.asarray(freq[None, :], jnp.float32)
    kv, cosine, sine = pl.pallas_call(
        key_kernel,
        out_shape=[
            shape((2 * rows, HEAD), jnp.bfloat16),
            shape((rows, HEAD), jnp.float32),
            shape((rows, HEAD), jnp.float32),
        ],
        in_specs=[HBM] * 5,
        out_specs=[VMEM] * 3,
        scratch_shapes=[
            pltpu.VMEM((rows, HEAD), jnp.bfloat16),
            pltpu.VMEM((1, HEAD), jnp.float32),
            pltpu.VMEM((1, rows), jnp.int32),
            pltpu.VMEM((1, HEAD), jnp.float32),
            pltpu.SemaphoreType.DMA((5,)),
        ],
        cost_estimate=COST,
        name="rotate_keys",
    )(keys, values, key_norm_gain[None, :], positions[None, :], freq)

    half = period // 2
    across = move(kv, lambda z: (z + half if z >= half else z - half) if z < period else None)
    inside = move(
        kv, lambda z: z + half if z < half else (z - half if z < period and z % 2 == 0 else None)
    )
    beneath = move(kv, lambda z: z + 1 if period <= z < depth - 1 else None)

    query = pl.pallas_call(
        query_kernel,
        out_shape=shape((heads * rows + PAD, HEAD), jnp.bfloat16),
        in_specs=[HBM] * 6,
        out_specs=VMEM,
        scratch_shapes=[
            pltpu.VMEM((rows, heads * HEAD), jnp.bfloat16),
            pltpu.VMEM((1, HEAD), jnp.float32),
            pltpu.VMEM((rows, HEAD), jnp.float32),
            pltpu.VMEM((rows, HEAD), jnp.float32),
            pltpu.VMEM(block_mask.shape, jnp.int32),
            pltpu.VMEM((1, rows), jnp.int32),
            pltpu.SemaphoreType.DMA((6,)),
        ],
        cost_estimate=COST,
        name="rotate_queries",
    )(queries, query_norm_gain[None, :], cosine, sine, block_mask, positions[None, :])
    query_cross = swap(query)

    def number(offset):
        return (plane + offset) % period * 2 + lane

    odd = plane % 2
    numbers = [mine, mine + 1 - 2 * lane, mine, mine - 2]
    numbers += [number(0), number(4), number(-1), number(3), number(1), number(5)]
    numbers += [number(2 + 4 * odd), number(6 - 4 * odd)]
    numbers = jnp.stack(numbers).astype(jnp.int32)
    info_own = jnp.concatenate([numbers, block_mask.reshape(-1)])
    mask_cross = query_cross[heads * rows, :].astype(jnp.int32)
    info = jnp.concatenate([info_own, mask_cross])

    def attend(info, jobs, slots, queries_in, states, shards, counts, name):
        out_shape, scratch = [], []
        for job in jobs:
            sums = shape((heads * rows, 2 * HEAD), jnp.float32)
            if job["pack"]:
                scratch.append(pltpu.VMEM(sums.shape, sums.dtype))
                sums = shape((heads * rows + 2 * heads * rows // HEAD, HEAD), jnp.bfloat16)
            out_shape.append(sums)
        inputs = [info] + queries_in + states + shards
        return pl.pallas_call(
            functools.partial(
                attend_kernel,
                jobs=jobs,
                slots=slots,
                counts=counts,
                rows=rows,
                heads=heads,
                prompt=prompt,
            ),
            out_shape=out_shape,
            in_specs=[SMEM] + [VMEM] * (len(inputs) - 1),
            out_specs=[VMEM] * len(out_shape),
            scratch_shapes=scratch,
            cost_estimate=COST,
            compiler_params=PARAMS,
            name=name,
        )(*inputs)

    def job(lane, state, pack=False):
        return dict(lane=lane, state=state, pack=pack)

    near_slots = [(NEAR, True), (NEAR + 1, True)]
    (near_own,) = attend(
        info_own, [job(0, False)], near_slots[:1], [query], [], [kv], [1], "attend_near"
    )
    across, near_own = lax.optimization_barrier((across, near_own))
    first = pl.pallas_call(
        functools.partial(choose_kernel, period=period),
        out_shape=shape(kv.shape, kv.dtype),
        in_specs=[SMEM] + [VMEM] * 2,
        out_specs=VMEM,
        compiler_params=PARAMS,
        cost_estimate=pl.CostEstimate(flops=CHOOSE, bytes_accessed=1, transcendentals=0),
        name="choose_shard",
    )(numbers, inside, across)
    aside = [(z + half if z % 2 else z - half) % depth for z in range(depth)]
    second = move(first, lambda z: aside[z] if aside[z] >= period else None)
    (near_cross,) = attend(
        info, [job(1, False)], near_slots, [query_cross], [], [kv, beneath], [1, 1], "attend_near_cross"
    )
    second, near_cross = lax.optimization_barrier((second, near_cross))

    held = pl.pallas_call(
        functools.partial(hold_kernel, period=period),
        out_shape=shape((2 * 2 * rows, HEAD), jnp.bfloat16),
        in_specs=[SMEM] + [VMEM] * 3,
        out_specs=VMEM,
        compiler_params=PARAMS,
        cost_estimate=pl.CostEstimate(flops=10**10, bytes_accessed=10**8, transcendentals=0),
        name="hold_shards",
    )(numbers, kv, first, second)
    low = move(held, lambda z: z + 1 if z + 1 < depth else None)
    high = move(held, lambda z: z - 1 if not 1 <= z < half else None)
    skip = move(
        held, lambda z: None if z in (2, depth - 1) else (z + 2 if z % 2 else z - 2)
    )

    held_slots = [(HELD, False), (HELD + 1, False)]
    low_slots = [(LOW, False), (LOW + 1, False)]
    high_slots = [(HIGH, False), (HIGH + 1, False)]
    skip_slots = [(SKIP, False), (SKIP + 1, False)]
    (cross,) = attend(
        info, [job(1, True)], held_slots, [query_cross], [near_cross], [held], [2], "attend_held_cross"
    )
    (cross,) = attend(
        info,
        [job(1, True)],
        low_slots + high_slots,
        [query_cross],
        [cross],
        [low, high],
        [2, 2],
        "attend_next_cross",
    )
    (cross,) = attend(
        info, [job(1, True, True)], skip_slots, [query_cross], [cross], [skip], [2], "attend_last_cross"
    )
    other = swap(cross)
    (own,) = attend(
        info_own,
        [job(0, True)],
        held_slots + low_slots + high_slots + skip_slots + near_slots[1:],
        [query],
        [near_own],
        [held, low, high, skip, beneath],
        [2, 2, 2, 2, 1],
        "attend_own",
    )
    return pl.pallas_call(
        finish_kernel,
        out_shape=shape((rows, heads * HEAD), jnp.bfloat16),
        in_specs=[VMEM] * 2,
        out_specs=VMEM,
        compiler_params=PARAMS,
        cost_estimate=COST,
        name="finish",
    )(own, other)


def solution(mesh):
    return jax.shard_map(
        local,
        mesh=mesh,
        in_specs=(
            P(("dp", "ctx"), "tp"),
            P(("dp", "ctx"), "tp"),
            P(("dp", "ctx"), "tp"),
            P(),
            P(),
            P(("dp", "ctx")),
            P(("dp", "ctx")),
            P(("dp", "ctx"), None),
        ),
        out_specs=P(("dp", "ctx"), "tp"),
        check_vma=False,
    )
```

```python
import functools
import math

import jax
import jax.numpy as jnp
import numpy as np
from jax import lax
from jax.experimental import pallas as pl
from jax.experimental.pallas import tpu as pltpu
from jax.sharding import PartitionSpec as P

HEAD = 128
NT = (((1,), (1,)), ((), ()))
HBM = pl.BlockSpec(memory_space=pltpu.HBM)
VMEM = pl.BlockSpec(memory_space=pltpu.VMEM)
SMEM = pl.BlockSpec(memory_space=pltpu.SMEM)
PARAMS = pltpu.CompilerParams(vmem_limit_bytes=40 * 2**20)
COST = pl.CostEstimate(flops=1, bytes_accessed=1, transcendentals=0)
CHOOSE = 10**10
PAD = 16
PART = 128

NEAR, HELD, LOW, HIGH, SKIP, MASKS = 2, 4, 6, 8, 10, 12


def rotate(vec, gain, cosine, sine):
    vec = vec.astype(jnp.float32)
    vec = vec * lax.rsqrt(jnp.mean(vec * vec, axis=-1, keepdims=True) + 1e-06) * gain
    turned = jnp.concatenate([vec[:, HEAD // 2 :], vec[:, : HEAD // 2]], axis=1)
    return vec * cosine + turned * sine


def cos_sin(angle):
    turns = jnp.floor(angle * (2 / math.pi) + 0.5)
    rest = angle - turns * 1.5703125
    rest = rest - turns * 4.837512969970703e-4
    rest = rest - turns * 7.549789954891882e-8
    square = rest * rest
    sine = -1.9515295891e-4 * square + 8.3321608736e-3
    sine = (sine * square - 1.6666654611e-1) * square * rest + rest
    cosine = 2.443315711809948e-5 * square - 1.388731625493765e-3
    cosine = (cosine * square + 4.166664568298827e-2) * square * square - 0.5 * square + 1.0
    quarter = turns.astype(jnp.int32)
    odd = (quarter & 1) == 1
    swapped_sine = jnp.where(odd, cosine, sine)
    swapped_cosine = jnp.where(odd, sine, cosine)
    sine = jnp.where((quarter & 2) == 2, -swapped_sine, swapped_sine)
    cosine = jnp.where(((quarter + 1) & 2) == 2, -swapped_cosine, swapped_cosine)
    return cosine, sine


def key_kernel(keys, values, gain, positions, freq, out, cosine, sine, key_at, gain_at, pos_at, freq_at, sems):
    rows = keys.shape[0]
    copies = [
        pltpu.make_async_copy(source, target, sems.at[i])
        for i, (source, target) in enumerate(
            [
                (positions, pos_at),
                (freq, freq_at),
                (keys, key_at),
                (gain, gain_at),
                (values, out.at[pl.ds(rows, rows), :]),
            ]
        )
    ]
    for copy in copies:
        copy.start()
    copies[0].wait()
    copies[1].wait()
    place = jnp.broadcast_to(pos_at[...].astype(jnp.float32), (HEAD, rows)).T
    cos, sin = cos_sin(place * freq_at[...])
    lane = lax.broadcasted_iota(jnp.int32, (rows, HEAD), 1)
    sin = jnp.where(lane < HEAD // 2, -sin, sin)
    cosine[...] = cos
    sine[...] = sin
    copies[2].wait()
    copies[3].wait()
    out[:rows, :] = rotate(key_at[...], gain_at[...], cos, sin).astype(out.dtype)
    copies[4].wait()


def query_kernel(
    queries, gain, cosine, sine, mask, positions, out, query_at, gain_at, cos_at, sin_at, mask_at, pos_at, sems
):
    rows = queries.shape[0]
    heads = queries.shape[1] // HEAD
    sources = [mask, positions, gain, cosine, sine, queries]
    targets = [mask_at, pos_at, gain_at, cos_at, sin_at, query_at]
    copies = [
        pltpu.make_async_copy(source, target, sems.at[i])
        for i, (source, target) in enumerate(zip(sources, targets))
    ]
    for copy in copies:
        copy.start()
    copies[0].wait()
    copies[1].wait()
    line = mask_at[...].astype(jnp.float32)
    place = pos_at[...]
    high = (place >> 7).astype(jnp.float32)
    low = (place & (PART - 1)).astype(jnp.float32)
    lines = [jnp.concatenate([line[:1, :], line[1:, :]], axis=1)]
    lines += [part[:, at : at + HEAD] for part in (high, low) for at in range(0, rows, HEAD)]
    lines += [jnp.zeros((PAD - len(lines), HEAD), jnp.float32)]
    out[heads * rows :, :] = jnp.concatenate(lines, axis=0).astype(out.dtype)
    for copy in copies[2:]:
        copy.wait()
    for head in range(heads):
        part = query_at[:, head * HEAD : (head + 1) * HEAD]
        out[head * rows : (head + 1) * rows, :] = rotate(
            part, gain_at[...], cos_at[...], sin_at[...]
        ).astype(out.dtype)


def choose_kernel(info, inside, across, out, *, period):
    @pl.when(info[0] // 2 < period)
    def _():
        out[...] = inside[...]

    @pl.when(info[0] // 2 >= period)
    def _():
        out[...] = across[...]


def hold_kernel(info, own, opposite, second, held, *, period):
    size = own.shape[0]

    @pl.when(info[0] // 2 < period)
    def _():
        held[:size, :] = own[...]

    @pl.when(info[0] // 2 >= period)
    def _():
        held[:size, :] = second[...]

    held[size:, :] = opposite[...]


def attend_kernel(info, *refs, jobs, slots, counts, rows, heads, span, prompt):
    refs = list(refs)
    queries = [refs.pop(0) for _ in jobs]
    states = [refs.pop(0) if job["state"] else None for job in jobs]
    shards = []
    for count in counts:
        ref = refs.pop(0)
        shards += [(ref, part * 2 * rows) for part in range(count)]
    half = rows // 2
    begin, end = span
    scale = HEAD**-0.5 * math.log2(math.e)
    ones = jnp.ones((rows, HEAD), jnp.bfloat16)

    def partial(query, head, shard, mask):
        ref, at = shard
        score = lax.dot_general(
            query[pl.ds(head * rows, rows), :],
            ref[at : at + rows, :],
            NT,
            preferred_element_type=jnp.float32,
        )
        weight = jnp.exp2(score * scale)
        if mask is not None:
            weight = jnp.where(mask, weight, 0.0)
        extended = jnp.concatenate([ref[at + rows : at + 2 * rows, :], ones], axis=1)
        return jnp.dot(weight.astype(jnp.bfloat16), extended, preferred_element_type=jnp.float32)

    for job, query, state in zip(jobs, queries, states):
        out = refs.pop(0)
        total = refs.pop() if job["pack"] else out
        lane = job["lane"]
        mine = info[lane]

        def block(shard, a, b, lane=lane):
            width = 4 * prompt // rows
            return info[MASKS + lane * 2 * width + a * width + 2 * shard + b]

        early, late = [], []
        for (slot, near), shard in zip(slots, shards):
            number = info[slot]
            seen = [block(number, a, b) > 0 for a in range(2) for b in range(2)]
            any_seen = seen[0] | seen[1] | seen[2] | seen[3]
            if near:
                late.append((shard, number, any_seen & (number * rows >= prompt)))
            else:
                all_seen = seen[0] & seen[1] & seen[2] & seen[3]
                all_seen = all_seen & (number < mine) & (number * rows < prompt)
                early.append((shard, number, any_seen, all_seen))

        def add(shard, mask, query=query, total=total):
            @pl.loop(0, (end - begin) // 4)
            def _(group):
                for inner in range(4):
                    head = group * 4 + inner
                    at = pl.ds(pl.multiple_of(head * rows, rows), rows)
                    total[at, :] += partial(query, begin + head, shard, mask)

        def add_masked(shard, number, near, add=add, block=block, query=query, mine=mine):
            row = lax.broadcasted_iota(jnp.int32, (rows, rows), 0)
            column = lax.broadcasted_iota(jnp.int32, (rows, rows), 1)
            upper = jnp.where(column < half, block(number, 0, 0), block(number, 0, 1))
            lower = jnp.where(column < half, block(number, 1, 0), block(number, 1, 1))
            key = number * rows + column
            mask = (jnp.where(row < half, upper, lower) > 0) & (key <= mine * rows + row)
            if near:
                lines = query[heads * rows :, :].astype(jnp.float32)
                count = rows // HEAD
                place = jnp.concatenate(
                    [lines[1 + i : 2 + i, :] * PART + lines[1 + count + i : 2 + count + i, :] for i in range(count)],
                    axis=1,
                )
                offset = jnp.broadcast_to(place - prompt, (rows, rows)).T.astype(jnp.int32)
                mask = mask & ((key < prompt) | (key >= mine * rows + row - offset))
            add(shard, mask)

        def together(query=query, state=state, total=total, early=early):
            for head in range(begin, end):
                sums = None if state is None else state[head * rows : (head + 1) * rows, :]
                for shard, *_ in early:
                    new = partial(query, head, shard, None)
                    sums = new if sums is None else sums + new
                total[(head - begin) * rows : (head - begin + 1) * rows, :] = sums

        def one_by_one(state=state, total=total, early=early, add=add, add_masked=add_masked):
            total[...] = jnp.zeros_like(total) if state is None else state[begin * rows : end * rows, :]
            for shard, number, any_seen, all_seen in early:
                pl.when(all_seen)(functools.partial(add, shard, None))
                pl.when(any_seen & jnp.logical_not(all_seen))(
                    functools.partial(add_masked, shard, number, False)
                )

        if early:
            all_full = functools.reduce(jnp.logical_and, [entry[3] for entry in early])
            pl.when(all_full)(together)
            pl.when(jnp.logical_not(all_full))(one_by_one)
        else:
            one_by_one()
        for shard, number, any_seen in late:
            pl.when(any_seen)(functools.partial(add_masked, shard, number, True))

        if job["pack"]:
            count = end - begin
            at_lane = lax.broadcasted_iota(jnp.int32, (rows, HEAD), 1)
            packed = jnp.zeros((rows, HEAD), jnp.float32)
            for head in range(count):
                at = pl.ds(head * rows, rows)
                out[at, :] = total[at, :HEAD].astype(out.dtype)
                whole = total[at, HEAD:]
                high = whole.astype(jnp.bfloat16).astype(jnp.float32)
                packed = jnp.where(at_lane == head, high, packed)
                packed = jnp.where(at_lane == count + head, whole - high, packed)
            turned = packed.T[: 2 * count, :]
            turned = [turned[:, at : at + HEAD] for at in range(0, rows, HEAD)]
            out[count * rows :, :] = jnp.concatenate(turned, axis=0).astype(out.dtype)


def finish_kernel(own, *refs):
    *others, out = refs
    rows = out.shape[0]
    count = out.shape[1] // HEAD // len(others)
    source = lax.broadcasted_iota(jnp.int32, (2 * count, HEAD), 0)
    for part, other in enumerate(others):
        packed = other[count * rows :, :].astype(jnp.float32)
        packed = [packed[at : at + 2 * count, :] for at in range(0, packed.shape[0], 2 * count)]
        packed = jnp.concatenate(packed, axis=1).astype(jnp.bfloat16)
        for head in range(count):
            at = slice(head * rows, (head + 1) * rows)
            own_at = slice((part * count + head) * rows, (part * count + head + 1) * rows)
            pick = jnp.where((source == head) | (source == count + head), 1.0, 0.0)
            total = lax.dot_general(
                packed,
                pick.astype(jnp.bfloat16),
                (((0,), (0,)), ((), ())),
                preferred_element_type=jnp.float32,
            )
            total = total + own[own_at, HEAD:]
            value = own[own_at, :HEAD] + other[at, :].astype(jnp.float32)
            lanes = slice((part * count + head) * HEAD, (part * count + head + 1) * HEAD)
            out[:, lanes] = (value / total).astype(out.dtype)


def local(
    queries, keys, values, query_norm_gain, key_norm_gain, positions, segment_ids, block_mask
):
    rows = queries.shape[0]
    heads = queries.shape[1] // HEAD
    ring = lax.axis_size("ctx")
    mine = lax.axis_index("ctx")
    prompt = ring * rows // 2
    depth = ring // 2
    period = depth // 2
    plane, lane = mine // 2, mine % 2
    shape = jax.ShapeDtypeStruct

    def move(array, target):
        pairs = [(z * 2 + y, target(z) % depth * 2 + y) for z in range(depth) for y in range(2) if target(z) is not None]
        return lax.ppermute(array, "ctx", pairs)

    def swap(array):
        return lax.ppermute(array, "ctx", [(c, c ^ 1) for c in range(ring)])

    freq = 1000000.0 ** (-2.0 * (np.arange(HEAD) % (HEAD // 2)) / HEAD)
    freq = jnp.asarray(freq[None, :], jnp.float32)
    kv, cosine, sine = pl.pallas_call(
        key_kernel,
        out_shape=[
            shape((2 * rows, HEAD), jnp.bfloat16),
            shape((rows, HEAD), jnp.float32),
            shape((rows, HEAD), jnp.float32),
        ],
        in_specs=[HBM] * 5,
        out_specs=[VMEM] * 3,
        scratch_shapes=[
            pltpu.VMEM((rows, HEAD), jnp.bfloat16),
            pltpu.VMEM((1, HEAD), jnp.float32),
            pltpu.VMEM((1, rows), jnp.int32),
            pltpu.VMEM((1, HEAD), jnp.float32),
            pltpu.SemaphoreType.DMA((5,)),
        ],
        cost_estimate=COST,
        name="rotate_keys",
    )(keys, values, key_norm_gain[None, :], positions[None, :], freq)

    half = period // 2
    across = move(kv, lambda z: (z + half if z >= half else z - half) if z < period else None)
    inside = move(
        kv, lambda z: z + half if z < half else (z - half if z < period and z % 2 == 0 else None)
    )
    beneath = move(kv, lambda z: z + 1 if period <= z < depth - 1 else None)

    query = pl.pallas_call(
        query_kernel,
        out_shape=shape((heads * rows + PAD, HEAD), jnp.bfloat16),
        in_specs=[HBM] * 6,
        out_specs=VMEM,
        scratch_shapes=[
            pltpu.VMEM((rows, heads * HEAD), jnp.bfloat16),
            pltpu.VMEM((1, HEAD), jnp.float32),
            pltpu.VMEM((rows, HEAD), jnp.float32),
            pltpu.VMEM((rows, HEAD), jnp.float32),
            pltpu.VMEM(block_mask.shape, jnp.int32),
            pltpu.VMEM((1, rows), jnp.int32),
            pltpu.SemaphoreType.DMA((6,)),
        ],
        cost_estimate=COST,
        name="rotate_queries",
    )(queries, query_norm_gain[None, :], cosine, sine, block_mask, positions[None, :])
    query_cross = swap(query)

    def number(offset):
        return (plane + offset) % period * 2 + lane

    odd = plane % 2
    numbers = [mine, mine + 1 - 2 * lane, mine, mine - 2]
    numbers += [number(0), number(4), number(-1), number(3), number(1), number(5)]
    numbers += [number(2 + 4 * odd), number(6 - 4 * odd)]
    numbers = jnp.stack(numbers).astype(jnp.int32)
    info_own = jnp.concatenate([numbers, block_mask.reshape(-1)])
    mask_cross = query_cross[heads * rows, :].astype(jnp.int32)
    info = jnp.concatenate([info_own, mask_cross])

    def attend(info, jobs, slots, queries_in, states, shards, counts, name, span=(0, heads)):
        out_shape, scratch = [], []
        size = (span[1] - span[0]) * rows
        for job in jobs:
            sums = shape((size, 2 * HEAD), jnp.float32)
            if job["pack"]:
                scratch.append(pltpu.VMEM(sums.shape, sums.dtype))
                sums = shape((size + 2 * size // HEAD, HEAD), jnp.bfloat16)
            out_shape.append(sums)
        inputs = [info] + queries_in + states + shards
        return pl.pallas_call(
            functools.partial(
                attend_kernel,
                jobs=jobs,
                slots=slots,
                counts=counts,
                rows=rows,
                heads=heads,
                span=span,
                prompt=prompt,
            ),
            out_shape=out_shape,
            in_specs=[SMEM] + [VMEM] * (len(inputs) - 1),
            out_specs=[VMEM] * len(out_shape),
            scratch_shapes=scratch,
            cost_estimate=COST,
            compiler_params=PARAMS,
            name=name,
        )(*inputs)

    def job(lane, state, pack=False):
        return dict(lane=lane, state=state, pack=pack)

    near_slots = [(NEAR, True), (NEAR + 1, True)]
    inside, query_own = lax.optimization_barrier((inside, query))
    (near_own,) = attend(
        info_own, [job(0, False)], near_slots[:1], [query_own], [], [kv], [1], "attend_near"
    )
    across, near_own = lax.optimization_barrier((across, near_own))
    first = pl.pallas_call(
        functools.partial(choose_kernel, period=period),
        out_shape=shape(kv.shape, kv.dtype),
        in_specs=[SMEM] + [VMEM] * 2,
        out_specs=VMEM,
        compiler_params=PARAMS,
        cost_estimate=pl.CostEstimate(flops=CHOOSE, bytes_accessed=1, transcendentals=0),
        name="choose_shard",
    )(numbers, inside, across)
    aside = [(z + half if z % 2 else z - half) % depth for z in range(depth)]
    second = move(first, lambda z: aside[z] if aside[z] >= period else None)
    (near_cross,) = attend(
        info, [job(1, False)], near_slots, [query_cross], [], [kv, beneath], [1, 1], "attend_near_cross"
    )
    second, near_cross = lax.optimization_barrier((second, near_cross))

    held = pl.pallas_call(
        functools.partial(hold_kernel, period=period),
        out_shape=shape((2 * 2 * rows, HEAD), jnp.bfloat16),
        in_specs=[SMEM] + [VMEM] * 3,
        out_specs=VMEM,
        compiler_params=PARAMS,
        cost_estimate=pl.CostEstimate(flops=10**10, bytes_accessed=10**8, transcendentals=0),
        name="hold_shards",
    )(numbers, kv, first, second)
    low = move(held, lambda z: z + 1 if z + 1 < depth else None)
    high = move(held, lambda z: z - 1 if not 1 <= z < half else None)
    skip = move(
        held, lambda z: None if z in (2, depth - 1) else (z + 2 if z % 2 else z - 2)
    )

    held_slots = [(HELD, False), (HELD + 1, False)]
    low_slots = [(LOW, False), (LOW + 1, False)]
    high_slots = [(HIGH, False), (HIGH + 1, False)]
    skip_slots = [(SKIP, False), (SKIP + 1, False)]
    (cross,) = attend(
        info, [job(1, True)], held_slots, [query_cross], [near_cross], [held], [2], "attend_held_cross"
    )
    (cross,) = attend(
        info,
        [job(1, True)],
        skip_slots + low_slots,
        [query_cross],
        [cross],
        [skip, low],
        [2, 2],
        "attend_next_cross",
    )
    (cross,) = attend(
        info, [job(1, True, True)], high_slots, [query_cross], [cross], [high], [2], "attend_last_cross"
    )
    other = swap(cross)
    (own,) = attend(
        info_own,
        [job(0, True)],
        held_slots + low_slots + high_slots + skip_slots + near_slots[1:],
        [query],
        [near_own],
        [held, low, high, skip, beneath],
        [2, 2, 2, 2, 1],
        "attend_own",
    )
    return pl.pallas_call(
        finish_kernel,
        out_shape=shape((rows, heads * HEAD), jnp.bfloat16),
        in_specs=[VMEM] * 2,
        out_specs=VMEM,
        compiler_params=PARAMS,
        cost_estimate=COST,
        name="finish",
    )(own, other)


def solution(mesh):
    return jax.shard_map(
        local,
        mesh=mesh,
        in_specs=(
            P(("dp", "ctx"), "tp"),
            P(("dp", "ctx"), "tp"),
            P(("dp", "ctx"), "tp"),
            P(),
            P(),
            P(("dp", "ctx")),
            P(("dp", "ctx")),
            P(("dp", "ctx"), None),
        ),
        out_specs=P(("dp", "ctx"), "tp"),
        check_vma=False,
    )
```

```python
import functools
import math

import jax
import jax.numpy as jnp
import numpy as np
from jax import lax
from jax.experimental import pallas as pl
from jax.experimental.pallas import tpu as pltpu
from jax.sharding import PartitionSpec as P

HEAD = 128
NT = (((1,), (1,)), ((), ()))
HBM = pl.BlockSpec(memory_space=pltpu.HBM)
VMEM = pl.BlockSpec(memory_space=pltpu.VMEM)
SMEM = pl.BlockSpec(memory_space=pltpu.SMEM)
PARAMS = pltpu.CompilerParams(vmem_limit_bytes=40 * 2**20)
COST = pl.CostEstimate(flops=1, bytes_accessed=1, transcendentals=0)
CHOOSE = 10**10
PAD = 16
PART = 128

NEAR, HELD, LOW, HIGH, SKIP, MASKS = 2, 4, 6, 8, 10, 12


def rotate(vec, gain, cosine, sine):
    vec = vec.astype(jnp.float32)
    vec = vec * lax.rsqrt(jnp.mean(vec * vec, axis=-1, keepdims=True) + 1e-06) * gain
    turned = jnp.concatenate([vec[:, HEAD // 2 :], vec[:, : HEAD // 2]], axis=1)
    return vec * cosine + turned * sine


def cos_sin(angle):
    turns = jnp.floor(angle * (2 / math.pi) + 0.5)
    rest = angle - turns * 1.5703125
    rest = rest - turns * 4.837512969970703e-4
    rest = rest - turns * 7.549789954891882e-8
    square = rest * rest
    sine = -1.9515295891e-4 * square + 8.3321608736e-3
    sine = (sine * square - 1.6666654611e-1) * square * rest + rest
    cosine = 2.443315711809948e-5 * square - 1.388731625493765e-3
    cosine = (cosine * square + 4.166664568298827e-2) * square * square - 0.5 * square + 1.0
    quarter = turns.astype(jnp.int32)
    odd = (quarter & 1) == 1
    swapped_sine = jnp.where(odd, cosine, sine)
    swapped_cosine = jnp.where(odd, sine, cosine)
    sine = jnp.where((quarter & 2) == 2, -swapped_sine, swapped_sine)
    cosine = jnp.where(((quarter + 1) & 2) == 2, -swapped_cosine, swapped_cosine)
    return cosine, sine


def key_kernel(keys, values, gain, positions, freq, out, cosine, sine, key_at, gain_at, pos_at, freq_at, sems):
    rows = keys.shape[0]
    copies = [
        pltpu.make_async_copy(source, target, sems.at[i])
        for i, (source, target) in enumerate(
            [
                (positions, pos_at),
                (freq, freq_at),
                (keys, key_at),
                (gain, gain_at),
                (values, out.at[pl.ds(rows, rows), :]),
            ]
        )
    ]
    for copy in copies:
        copy.start()
    copies[0].wait()
    copies[1].wait()
    place = jnp.broadcast_to(pos_at[...].astype(jnp.float32), (HEAD, rows)).T
    cos, sin = cos_sin(place * freq_at[...])
    lane = lax.broadcasted_iota(jnp.int32, (rows, HEAD), 1)
    sin = jnp.where(lane < HEAD // 2, -sin, sin)
    cosine[...] = cos
    sine[...] = sin
    copies[2].wait()
    copies[3].wait()
    out[:rows, :] = rotate(key_at[...], gain_at[...], cos, sin).astype(out.dtype)
    copies[4].wait()


def query_kernel(
    queries, gain, cosine, sine, mask, positions, out, query_at, gain_at, cos_at, sin_at, mask_at, pos_at, sems
):
    rows = queries.shape[0]
    heads = queries.shape[1] // HEAD
    sources = [mask, positions, gain, cosine, sine, queries]
    targets = [mask_at, pos_at, gain_at, cos_at, sin_at, query_at]
    copies = [
        pltpu.make_async_copy(source, target, sems.at[i])
        for i, (source, target) in enumerate(zip(sources, targets))
    ]
    for copy in copies:
        copy.start()
    copies[0].wait()
    copies[1].wait()
    line = mask_at[...].astype(jnp.float32)
    place = pos_at[...]
    high = (place >> 7).astype(jnp.float32)
    low = (place & (PART - 1)).astype(jnp.float32)
    lines = [jnp.concatenate([line[:1, :], line[1:, :]], axis=1)]
    lines += [part[:, at : at + HEAD] for part in (high, low) for at in range(0, rows, HEAD)]
    lines += [jnp.zeros((PAD - len(lines), HEAD), jnp.float32)]
    out[heads * rows :, :] = jnp.concatenate(lines, axis=0).astype(out.dtype)
    for copy in copies[2:]:
        copy.wait()
    for head in range(heads):
        part = query_at[:, head * HEAD : (head + 1) * HEAD]
        out[head * rows : (head + 1) * rows, :] = rotate(
            part, gain_at[...], cos_at[...], sin_at[...]
        ).astype(out.dtype)


def choose_kernel(info, inside, across, out, *, period):
    @pl.when(info[0] // 2 < period)
    def _():
        out[...] = inside[...]

    @pl.when(info[0] // 2 >= period)
    def _():
        out[...] = across[...]


def hold_kernel(info, own, opposite, second, held, *, period):
    size = own.shape[0]

    @pl.when(info[0] // 2 < period)
    def _():
        held[:size, :] = own[...]

    @pl.when(info[0] // 2 >= period)
    def _():
        held[:size, :] = second[...]

    held[size:, :] = opposite[...]


def attend_kernel(info, *refs, jobs, slots, counts, rows, heads, span, prompt):
    refs = list(refs)
    queries = [refs.pop(0) for _ in jobs]
    states = [refs.pop(0) if job["state"] else None for job in jobs]
    shards = []
    for count in counts:
        ref = refs.pop(0)
        shards += [(ref, part * 2 * rows) for part in range(count)]
    half = rows // 2
    begin, end = span
    scale = HEAD**-0.5 * math.log2(math.e)
    ones = jnp.ones((rows, HEAD), jnp.bfloat16)

    def partial(query, head, shard, mask):
        ref, at = shard
        score = lax.dot_general(
            query[pl.ds(head * rows, rows), :],
            ref[at : at + rows, :],
            NT,
            preferred_element_type=jnp.float32,
        )
        weight = jnp.exp2(score * scale)
        if mask is not None:
            weight = jnp.where(mask, weight, 0.0)
        extended = jnp.concatenate([ref[at + rows : at + 2 * rows, :], ones], axis=1)
        return jnp.dot(weight.astype(jnp.bfloat16), extended, preferred_element_type=jnp.float32)

    for job, query, state in zip(jobs, queries, states):
        out = refs.pop(0)
        total = refs.pop() if job["pack"] else out
        lane = job["lane"]
        mine = info[lane]

        def block(shard, a, b, lane=lane):
            width = 4 * prompt // rows
            return info[MASKS + lane * 2 * width + a * width + 2 * shard + b]

        early, late = [], []
        for (slot, near), shard in zip(slots, shards):
            number = info[slot]
            seen = [block(number, a, b) > 0 for a in range(2) for b in range(2)]
            any_seen = seen[0] | seen[1] | seen[2] | seen[3]
            if near:
                late.append((shard, number, any_seen))
            else:
                all_seen = seen[0] & seen[1] & seen[2] & seen[3]
                all_seen = all_seen & (number < mine) & (number * rows < prompt)
                early.append((shard, number, any_seen, all_seen))

        def add(shard, mask, query=query, total=total):
            @pl.loop(0, (end - begin) // 4)
            def _(group):
                for inner in range(4):
                    head = group * 4 + inner
                    at = pl.ds(pl.multiple_of(head * rows, rows), rows)
                    total[at, :] += partial(query, begin + head, shard, mask)

        def add_masked(shard, number, near, add=add, block=block, query=query, mine=mine):
            row = lax.broadcasted_iota(jnp.int32, (rows, rows), 0)
            column = lax.broadcasted_iota(jnp.int32, (rows, rows), 1)
            upper = jnp.where(column < half, block(number, 0, 0), block(number, 0, 1))
            lower = jnp.where(column < half, block(number, 1, 0), block(number, 1, 1))
            key = number * rows + column
            mask = (jnp.where(row < half, upper, lower) > 0) & (key <= mine * rows + row)
            if near:
                lines = query[heads * rows :, :].astype(jnp.float32)
                count = rows // HEAD
                place = jnp.concatenate(
                    [lines[1 + i : 2 + i, :] * PART + lines[1 + count + i : 2 + count + i, :] for i in range(count)],
                    axis=1,
                )
                offset = jnp.broadcast_to(place - prompt, (rows, rows)).T.astype(jnp.int32)
                mask = mask & ((key < prompt) | (key >= mine * rows + row - offset))
            add(shard, mask)

        def together(query=query, state=state, total=total, early=early):
            for head in range(begin, end):
                sums = None if state is None else state[head * rows : (head + 1) * rows, :]
                for shard, *_ in early:
                    new = partial(query, head, shard, None)
                    sums = new if sums is None else sums + new
                total[(head - begin) * rows : (head - begin + 1) * rows, :] = sums

        def one_by_one(state=state, total=total, early=early, add=add, add_masked=add_masked):
            total[...] = jnp.zeros_like(total) if state is None else state[begin * rows : end * rows, :]
            for shard, number, any_seen, all_seen in early:
                pl.when(all_seen)(functools.partial(add, shard, None))
                pl.when(any_seen & jnp.logical_not(all_seen))(
                    functools.partial(add_masked, shard, number, False)
                )

        if early:
            all_full = functools.reduce(jnp.logical_and, [entry[3] for entry in early])
            pl.when(all_full)(together)
            pl.when(jnp.logical_not(all_full))(one_by_one)
        else:
            one_by_one()
        for shard, number, any_seen in late:
            pl.when(any_seen)(functools.partial(add_masked, shard, number, True))

        if job["pack"]:
            count = end - begin
            at_lane = lax.broadcasted_iota(jnp.int32, (rows, HEAD), 1)
            packed = jnp.zeros((rows, HEAD), jnp.float32)
            for head in range(count):
                at = pl.ds(head * rows, rows)
                out[at, :] = total[at, :HEAD].astype(out.dtype)
                whole = total[at, HEAD:]
                high = whole.astype(jnp.bfloat16).astype(jnp.float32)
                packed = jnp.where(at_lane == head, high, packed)
                packed = jnp.where(at_lane == count + head, whole - high, packed)
            turned = packed.T[: 2 * count, :]
            turned = [turned[:, at : at + HEAD] for at in range(0, rows, HEAD)]
            out[count * rows :, :] = jnp.concatenate(turned, axis=0).astype(out.dtype)


def finish_kernel(own, *refs):
    *others, out = refs
    rows = out.shape[0]
    count = out.shape[1] // HEAD // len(others)
    source = lax.broadcasted_iota(jnp.int32, (2 * count, HEAD), 0)
    for part, other in enumerate(others):
        packed = other[count * rows :, :].astype(jnp.float32)
        packed = [packed[at : at + 2 * count, :] for at in range(0, packed.shape[0], 2 * count)]
        packed = jnp.concatenate(packed, axis=1).astype(jnp.bfloat16)
        for head in range(count):
            at = slice(head * rows, (head + 1) * rows)
            own_at = slice((part * count + head) * rows, (part * count + head + 1) * rows)
            pick = jnp.where((source == head) | (source == count + head), 1.0, 0.0)
            total = lax.dot_general(
                packed,
                pick.astype(jnp.bfloat16),
                (((0,), (0,)), ((), ())),
                preferred_element_type=jnp.float32,
            )
            total = total + own[own_at, HEAD:]
            value = own[own_at, :HEAD] + other[at, :].astype(jnp.float32)
            lanes = slice((part * count + head) * HEAD, (part * count + head + 1) * HEAD)
            out[:, lanes] = (value / total).astype(out.dtype)


def local(
    queries, keys, values, query_norm_gain, key_norm_gain, positions, segment_ids, block_mask
):
    rows = queries.shape[0]
    heads = queries.shape[1] // HEAD
    ring = lax.axis_size("ctx")
    mine = lax.axis_index("ctx")
    prompt = ring * rows // 2
    depth = ring // 2
    period = depth // 2
    plane, lane = mine // 2, mine % 2
    shape = jax.ShapeDtypeStruct

    def move(array, target):
        pairs = [(z * 2 + y, target(z) % depth * 2 + y) for z in range(depth) for y in range(2) if target(z) is not None]
        return lax.ppermute(array, "ctx", pairs)

    def swap(array):
        return lax.ppermute(array, "ctx", [(c, c ^ 1) for c in range(ring)])

    freq = 1000000.0 ** (-2.0 * (np.arange(HEAD) % (HEAD // 2)) / HEAD)
    freq = jnp.asarray(freq[None, :], jnp.float32)
    kv, cosine, sine = pl.pallas_call(
        key_kernel,
        out_shape=[
            shape((2 * rows, HEAD), jnp.bfloat16),
            shape((rows, HEAD), jnp.float32),
            shape((rows, HEAD), jnp.float32),
        ],
        in_specs=[HBM] * 5,
        out_specs=[VMEM] * 3,
        scratch_shapes=[
            pltpu.VMEM((rows, HEAD), jnp.bfloat16),
            pltpu.VMEM((1, HEAD), jnp.float32),
            pltpu.VMEM((1, rows), jnp.int32),
            pltpu.VMEM((1, HEAD), jnp.float32),
            pltpu.SemaphoreType.DMA((5,)),
        ],
        cost_estimate=COST,
        name="rotate_keys",
    )(keys, values, key_norm_gain[None, :], positions[None, :], freq)

    half = period // 2
    across = move(kv, lambda z: (z + half if z >= half else z - half) if z < period else None)
    inside = move(
        kv, lambda z: z + half if z < half else (z - half if z < period and z % 2 == 0 else None)
    )
    beneath = move(
        kv, lambda z: 2 if z == 0 else (z + 1 if period <= z < depth - 1 else None)
    )

    query = pl.pallas_call(
        query_kernel,
        out_shape=shape((heads * rows + PAD, HEAD), jnp.bfloat16),
        in_specs=[HBM] * 6,
        out_specs=VMEM,
        scratch_shapes=[
            pltpu.VMEM((rows, heads * HEAD), jnp.bfloat16),
            pltpu.VMEM((1, HEAD), jnp.float32),
            pltpu.VMEM((rows, HEAD), jnp.float32),
            pltpu.VMEM((rows, HEAD), jnp.float32),
            pltpu.VMEM(block_mask.shape, jnp.int32),
            pltpu.VMEM((1, rows), jnp.int32),
            pltpu.SemaphoreType.DMA((6,)),
        ],
        cost_estimate=COST,
        name="rotate_queries",
    )(queries, query_norm_gain[None, :], cosine, sine, block_mask, positions[None, :])
    query_cross = swap(query)

    def number(offset):
        return (plane + offset) % period * 2 + lane

    turned = ((plane % 2 == 1) | (plane == half + 2)).astype(jnp.int32)
    never = ring - 1
    second_near = jnp.where(plane == 2, lane, jnp.where(plane > period, mine - 2, never))

    def aslant(offset):
        return jnp.where(plane == 2, never, number(offset))

    numbers = [mine, mine + 1 - 2 * lane, jnp.where(plane < period, never, mine), second_near]
    numbers += [number(0), number(4), number(-1), number(3), number(1), number(5)]
    numbers += [aslant(2 + 4 * turned), aslant(6 - 4 * turned)]
    numbers = jnp.stack(numbers).astype(jnp.int32)
    info_own = jnp.concatenate([numbers, block_mask.reshape(-1)])
    mask_cross = query_cross[heads * rows, :].astype(jnp.int32)
    info = jnp.concatenate([info_own, mask_cross])

    def attend(info, jobs, slots, queries_in, states, shards, counts, name, span=(0, heads)):
        out_shape, scratch = [], []
        size = (span[1] - span[0]) * rows
        for job in jobs:
            sums = shape((size, 2 * HEAD), jnp.float32)
            if job["pack"]:
                scratch.append(pltpu.VMEM(sums.shape, sums.dtype))
                sums = shape((size + 2 * size // HEAD, HEAD), jnp.bfloat16)
            out_shape.append(sums)
        inputs = [info] + queries_in + states + shards
        return pl.pallas_call(
            functools.partial(
                attend_kernel,
                jobs=jobs,
                slots=slots,
                counts=counts,
                rows=rows,
                heads=heads,
                span=span,
                prompt=prompt,
            ),
            out_shape=out_shape,
            in_specs=[SMEM] + [VMEM] * (len(inputs) - 1),
            out_specs=[VMEM] * len(out_shape),
            scratch_shapes=scratch,
            cost_estimate=COST,
            compiler_params=PARAMS,
            name=name,
        )(*inputs)

    def job(lane, state, pack=False):
        return dict(lane=lane, state=state, pack=pack)

    near_slots = [(NEAR, True), (NEAR + 1, True)]
    inside, query_own = lax.optimization_barrier((inside, query))
    (near_own,) = attend(
        info_own, [job(0, False)], near_slots[:1], [query_own], [], [kv], [1], "attend_near"
    )
    across, near_own = lax.optimization_barrier((across, near_own))
    first = pl.pallas_call(
        functools.partial(choose_kernel, period=period),
        out_shape=shape(kv.shape, kv.dtype),
        in_specs=[SMEM] + [VMEM] * 2,
        out_specs=VMEM,
        compiler_params=PARAMS,
        cost_estimate=pl.CostEstimate(flops=CHOOSE, bytes_accessed=1, transcendentals=0),
        name="choose_shard",
    )(numbers, inside, across)
    aside = [(z + half if z % 2 else z - half) % depth for z in range(depth)]
    second = move(first, lambda z: aside[z] if aside[z] >= period else None)
    (near_cross,) = attend(
        info, [job(1, False)], near_slots, [query_cross], [], [kv, beneath], [1, 1], "attend_near_cross"
    )
    second, near_cross = lax.optimization_barrier((second, near_cross))

    held = pl.pallas_call(
        functools.partial(hold_kernel, period=period),
        out_shape=shape((2 * 2 * rows, HEAD), jnp.bfloat16),
        in_specs=[SMEM] + [VMEM] * 3,
        out_specs=VMEM,
        compiler_params=PARAMS,
        cost_estimate=pl.CostEstimate(flops=10**10, bytes_accessed=10**8, transcendentals=0),
        name="hold_shards",
    )(numbers, kv, first, second)
    low = move(held, lambda z: z + 1 if z + 1 < depth else None)
    high = move(held, lambda z: z - 1 if not 1 <= z < half else None)
    steps = {z: z + 2 if z % 2 or z == half else z - 2 for z in range(depth)}
    for unused in (2, period, depth - 1):
        del steps[unused]
    skip = move(held, steps.get)

    held_slots = [(HELD, False), (HELD + 1, False)]
    low_slots = [(LOW, False), (LOW + 1, False)]
    high_slots = [(HIGH, False), (HIGH + 1, False)]
    skip_slots = [(SKIP, False), (SKIP + 1, False)]
    (cross,) = attend(
        info, [job(1, True)], held_slots, [query_cross], [near_cross], [held], [2], "attend_held_cross"
    )
    (cross,) = attend(
        info,
        [job(1, True)],
        high_slots + low_slots,
        [query_cross],
        [cross],
        [high, low],
        [2, 2],
        "attend_next_cross",
    )
    (cross,) = attend(
        info, [job(1, True, True)], skip_slots, [query_cross], [cross], [skip], [2], "attend_last_cross"
    )
    other = swap(cross)
    (own,) = attend(
        info_own,
        [job(0, True)],
        held_slots + low_slots + high_slots + skip_slots + near_slots[1:],
        [query],
        [near_own],
        [held, low, high, skip, beneath],
        [2, 2, 2, 2, 1],
        "attend_own",
    )
    return pl.pallas_call(
        finish_kernel,
        out_shape=shape((rows, heads * HEAD), jnp.bfloat16),
        in_specs=[VMEM] * 2,
        out_specs=VMEM,
        compiler_params=PARAMS,
        cost_estimate=COST,
        name="finish",
    )(own, other)


def solution(mesh):
    return jax.shard_map(
        local,
        mesh=mesh,
        in_specs=(
            P(("dp", "ctx"), "tp"),
            P(("dp", "ctx"), "tp"),
            P(("dp", "ctx"), "tp"),
            P(),
            P(),
            P(("dp", "ctx")),
            P(("dp", "ctx")),
            P(("dp", "ctx"), None),
        ),
        out_specs=P(("dp", "ctx"), "tp"),
        check_vma=False,
    )
```
